32 devices in a mesh: section: 2 (over core), dp: 4 (over z), expert: 4 (over y, x).
Axes of the slice: x: 2, y: 2, z: 4, core: 2. Of those that a mesh axis runs over, the one named last changes fastest.
Arguments:
- ends: bfloat16 [2, 8192, 768], P('section', ('dp', 'expert')), may hold values from -6 to 6
- w_query: bfloat16 [2, 768, 768], P('section', 'dp'), may hold values from -0.21875 to 0.21875
- w_key: bfloat16 [2, 768, 768], P('section', 'dp'), may hold values from -0.21875 to 0.21875
- w_value: bfloat16 [2, 768, 768], P('section', 'dp'), may hold values from -0.21875 to 0.21875
- w_output: bfloat16 [2, 768, 768], P('section', 'dp'), may hold values from -1.25 to 1.25
- gain_attention: bfloat16 [2, 768], P('section', 'dp'), may hold values from 0.5 to 1.5
- gain_experts: bfloat16 [2, 768], P('section', 'dp'), may hold values from 0.5 to 1.5
- router: bfloat16 [2, 768, 4], P('section', 'dp'), may hold values from -0.15625 to 0.15625
- bias_table: bfloat16 [2, 32, 12], P('section', 'dp'), may hold values from -5 to 5
- experts_up: bfloat16 [2, 4, 768, 3072], P('section', 'expert', 'dp'), may hold values from -0.21875 to 0.21875
- experts_down: bfloat16 [2, 4, 3072, 768], P('section', 'expert', None, 'dp'), may hold values from -0.4375 to 0.4375
- routes: int32 [2, 8192], P('section', ('dp', 'expert')), may hold values from 0 to 3, as said below
- slots: int32 [2, 8192], P('section', ('dp', 'expert')), may hold values from 0 to 127, as said below
- segments: int32 [8192], P(('dp', 'expert')), may hold values from 0 to 8191, as said below
- buckets: int32 [511], replicated, may hold values from 0 to 31
Outputs:
- ends_out: bfloat16 [2, 8192, 768], P('section', ('dp', 'expert'))
- grad_w_query: float32 [2, 768, 768], P('section', 'dp')
- grad_w_key: float32 [2, 768, 768], P('section', 'dp')
- grad_w_value: float32 [2, 768, 768], P('section', 'dp')
- grad_w_output: float32 [2, 768, 768], P('section', 'dp')
- grad_gain_attention: float32 [2, 768], P('section', 'dp')
- grad_gain_experts: float32 [2, 768], P('section', 'dp')
- grad_router: float32 [2, 768, 4], P('section', 'dp')
- grad_bias_table: float32 [2, 32, 12], P('section', 'dp')
- grad_experts_up: float32 [2, 4, 768, 3072], P('section', 'expert', 'dp')
- grad_experts_down: float32 [2, 4, 3072, 768], P('section', 'expert', None, 'dp')
The draws below stay inside these ranges and needn't reach their ends.
Inputs may be any that keep to these rules, and one draw needn't show every extreme that they name: `routes`: blocks are the aligned runs of 256 tokens of one layer (one sequence each), ordered by layer, then device of dp+expert, then micro-batch. In a block, no expert is named by more than 128 tokens. For each layer, micro-batch and index of dp, one expert is named by exactly 128 tokens in every block of the 4 devices of that index. `slots`: within a block, no two tokens have the same route and slot. `segments`: A token's number is the index among all 8192 tokens of the last token of its document; never falling along each sequence of 256 tokens; a document never crosses a sequence's end.
All inputs are finite; a program needn't handle non-finite values.
Results may differ from the reference program's by a relative error of at most 0.028.
Values may be sent and summed in bfloat16 or wider, within the bound.
A program may use at most 192 MiB of HBM per device.

```python
import math
import jax
import jax.numpy as jnp
from jax import lax

D = 768
HEADS = 12
FF = 3072
NBUCK = 32
EXP_DEV = 1
MICRO = 2
SEQ = 256
EXPERTS = 4
CAP = 128
TOKENS = 8192


def route_pairs(key):
    blocks = 2 * TOKENS // SEQ
    per_layer = blocks // 2
    total_slots = EXPERTS * CAP
    row_count = EXPERTS // EXP_DEV
    key_tier, key_hot, key_noise, key_order = jax.random.split(key, 4)
    tiers = jax.random.randint(key_tier, (blocks, EXPERTS), 0, 4)
    block_ids = jnp.arange(blocks, dtype=jnp.int32)
    layer_ids = block_ids // per_layer
    inner = block_ids % per_layer
    device = inner // MICRO
    micro_id = inner % MICRO
    group_ids = (layer_ids * (per_layer // MICRO // row_count) + device // row_count) * MICRO + micro_id
    hot_table = jax.random.randint(key_hot, (blocks // row_count,), 0, EXPERTS)
    hottest = hot_table[group_ids]
    tiers = jnp.where(jnp.arange(EXPERTS, dtype=jnp.int32)[None, :] == hottest[:, None], 4, tiers)
    noise = jax.random.randint(key_noise, (blocks, EXPERTS, CAP), 0, 4096)
    position = jnp.arange(total_slots, dtype=jnp.int32).reshape(EXPERTS, CAP)
    score = ((tiers[:, :, None] * 4096 + noise) * total_slots + position[None]).reshape(blocks, total_slots)
    chosen = lax.top_k(score, SEQ)[1].astype(jnp.int32)
    shuffle = jax.random.randint(key_order, (blocks, SEQ), 0, 4096) * SEQ + jnp.arange(SEQ, dtype=jnp.int32)[None, :]
    order = jnp.argsort(shuffle, axis=1)
    picked = jnp.take_along_axis(chosen, order, axis=1)
    return ((picked // CAP).reshape(2, TOKENS).astype(jnp.int32), (picked % CAP).reshape(2, TOKENS).astype(jnp.int32))


def draw_routes(key, part):
    return route_pairs(key)[0]


def draw_slots(key, part):
    return route_pairs(key)[1]


def draw_segments(key, part):
    key = jax.random.fold_in(key, 7)
    count = TOKENS // SEQ
    shortest = max(1, SEQ * 2 // 5)
    pieces = SEQ // shortest + 2
    key_length, key_phase = jax.random.split(key)
    lengths = jax.random.randint(key_length, (count, pieces), shortest, 4 * SEQ + 1)
    phase = jax.random.randint(key_phase, (count, 1), 0, 4 * SEQ)
    bounds = jnp.cumsum(lengths, axis=1) - phase
    position = jnp.arange(SEQ, dtype=jnp.int32)
    later = jnp.where(bounds[:, None, :] > position[None, :, None], bounds[:, None, :], SEQ)
    closing = jnp.minimum(jnp.min(later, axis=-1), SEQ) - 1
    ids = closing + jnp.arange(count, dtype=jnp.int32)[:, None] * SEQ
    return ids.reshape(TOKENS).astype(jnp.int32)


def set_ends(result, stream_key, smallest, high):
    spot = [jax.random.randint(jax.random.fold_in(stream_key, axis), (), 0, length) for axis, length in enumerate(result.shape)]
    main_axis = result.shape.index(max(result.shape))
    neighbour = spot[:main_axis] + [(spot[main_axis] + 1) % result.shape[main_axis]] + spot[main_axis + 1:]
    return result.at[tuple(spot)].set(smallest).at[tuple(neighbour)].set(high)


def shard_levels(key, dims, cuts, low, top_value):
    level = 1.0
    for dim, blocks in cuts:
        draws = jax.random.uniform(jax.random.fold_in(jax.random.fold_in(key, 6), dim), (blocks,), jnp.float32, low / len(cuts), top_value / len(cuts))
        level = level * jnp.repeat(jnp.exp(draws), dims[dim] // blocks).reshape((-1,) + (1,) * (len(dims) - 1 - dim))
    return level


def gaussian(stream_key, shape, scale, reach, cuts=(), kind=jnp.bfloat16):
    entries = scale * jax.random.normal(stream_key, shape, jnp.float32)
    if cuts:
        entries = entries * shard_levels(stream_key, shape, cuts, -0.22, 0.18)
    return jnp.clip(entries, -reach, reach).astype(kind)


def setup_inputs(seed: int = 0) -> dict:
    key_list = jax.random.split(jax.random.key(seed), 16)
    ends = gaussian(key_list[0], (2, TOKENS, D), 1.0, 6.0, ((0, 2), (1, 16)))
    w_query = gaussian(key_list[1], (2, D, D), D ** -0.5, 0.21875, ((0, 2), (1, 4)))
    w_key = gaussian(key_list[2], (2, D, D), D ** -0.5, 0.21875, ((0, 2), (1, 4)))
    w_value = gaussian(key_list[3], (2, D, D), D ** -0.5, 0.21875, ((0, 2), (1, 4)))
    w_output = gaussian(key_list[4], (2, D, D), (D // 32) ** -0.5, 1.25, ((0, 2), (1, 4)))
    gain_attention = jnp.clip(1.0 + 0.1 * jax.random.normal(key_list[5], (2, D), jnp.float32), 0.5, 1.5).astype(jnp.bfloat16)
    gain_experts = jnp.clip(1.0 + 0.1 * jax.random.normal(key_list[6], (2, D), jnp.float32), 0.5, 1.5).astype(jnp.bfloat16)
    router = gaussian(key_list[7], (2, D, EXPERTS), (2 * D) ** -0.5, 0.15625, ((0, 2), (1, 4)))
    bias_table = gaussian(key_list[8], (2, NBUCK, HEADS), 1.0, 5.0, ((0, 2), (1, 4)))
    experts_up = gaussian(key_list[9], (2, EXPERTS, D, FF), D ** -0.5, 0.21875, ((0, 2), (1, 4), (2, 4)))
    experts_down = gaussian(key_list[10], (2, EXPERTS, FF, D), (max(FF // (EXPERTS * EXPERTS), 1)) ** -0.5, 0.4375, ((0, 2), (1, 4), (3, 4)))
    routes = draw_routes(jax.random.fold_in(key_list[15], 71), 0)
    slots = draw_slots(jax.random.fold_in(key_list[15], 71), 0)
    segments = draw_segments(jax.random.fold_in(key_list[15], 71), 0)
    buckets = set_ends(jax.random.randint(key_list[14], (2 * SEQ - 1,), 0, NBUCK), jax.random.fold_in(key_list[14], 1), 0, NBUCK - 1).astype(jnp.int32)
    return dict(ends=ends, w_query=w_query, w_key=w_key, w_value=w_value, w_output=w_output, gain_attention=gain_attention, gain_experts=gain_experts, router=router, bias_table=bias_table, experts_up=experts_up, experts_down=experts_down, routes=routes, slots=slots, segments=segments, buckets=buckets)


epsilon = 1e-06
highest = lax.Precision.HIGHEST

@jax.custom_vjp
def low(v):
    return lax.optimization_barrier(v.astype(jnp.bfloat16)).astype(jnp.float32)

@jax.custom_vjp
def low_back(v):
    return v

def low_keep(v):
    return (low(v), None)

def low_pass(kept, grad):
    return (grad,)

def back_keep(v):
    return (v, None)

def back_low(kept, grad):
    return (low(grad),)
low.defvjp(low_keep, low_pass)
low_back.defvjp(back_keep, back_low)

def normalize(values, gain):
    return values * lax.rsqrt(lax.optimization_barrier(jnp.mean(values * values, axis=-1, keepdims=True)) + epsilon) * gain

def layer(inputs, weights, route, slot, segment, bucket_index):
    query_w, key_w, value_w, output_w, gain_one, gain_two, router_w, table, up_w, down_w = weights
    length, model = inputs.shape
    heads = table.shape[1]
    width = model // heads
    normed = low(normalize(inputs, gain_one))

    def project(matrix):
        return low_back(low(jnp.dot(normed, matrix, precision=highest))).reshape(length, heads, width)
    queries = project(query_w)
    keys = project(key_w)
    values = project(value_w)
    bias = jnp.transpose(table[bucket_index], (2, 0, 1))
    scores = low_back(jnp.einsum('qhd,khd->hqk', queries, keys, precision=highest) * width ** (-0.5) + bias)
    same = segment[:, None] == segment[None, :]
    scores = jnp.where(same[None], scores, -1e+30)
    probs = jax.nn.softmax(scores, axis=-1)
    mixed = jnp.einsum('hqk,khd->qhd', low(probs), values, precision=highest).reshape(length, model)
    mixed = low_back(low(mixed))
    hidden = inputs + low_back(jnp.dot(mixed, output_w, precision=highest))
    routed = low(normalize(hidden, gain_two))
    experts = router_w.shape[1]
    capacity = 2 * length // experts
    chances = jax.nn.softmax(jnp.dot(routed, router_w, precision=highest), axis=-1)
    choose = (route[:, None] == jnp.arange(experts, dtype=jnp.int32)[None, :]).astype(jnp.float32)
    gate = lax.optimization_barrier(jnp.sum(chances * choose, axis=-1))
    target = (route * capacity + slot).astype(jnp.int32)
    buffer = jnp.zeros((experts * capacity, model), jnp.float32).at[target].add(routed)
    buffer = low_back(buffer).reshape(experts, capacity, model)
    before = low_back(jnp.einsum('ecd,edf->ecf', buffer, up_w, precision=highest))
    activated = low(jax.nn.gelu(before, approximate=False))
    after = low_back(low(jnp.einsum('ecf,efd->ecd', activated, down_w, precision=highest)))
    return hidden + gate[:, None] * after.reshape(experts * capacity, model)[target]

def two_layers(weights, inputs, route_pair, slot_pair, segment, bucket_index):
    lower = [matrix[0] for matrix in weights]
    upper = [matrix[1] for matrix in weights]
    middle = low_back(low(layer(inputs, lower, route_pair[0], slot_pair[0], segment, bucket_index)))
    return layer(middle, upper, route_pair[1], slot_pair[1], segment, bucket_index)

def reference(ends, w_query, w_key, w_value, w_output, gain_attention, gain_experts, router, bias_table, experts_up, experts_down, routes, slots, segments, buckets):
    weights = tuple((matrix.astype(jnp.float32) for matrix in (w_query, w_key, w_value, w_output, gain_attention, gain_experts, router, bias_table, experts_up, experts_down)))
    count = TOKENS // SEQ
    per_step = math.gcd(count, max(1, 4096 // SEQ))
    groups = count // per_step
    positions = jnp.arange(SEQ, dtype=jnp.int32)
    bucket_index = buckets[(positions[:, None] - positions[None, :] + SEQ - 1).astype(jnp.int32)]
    inputs = ends[0].astype(jnp.float32).reshape(groups, per_step, SEQ, D)
    cotangent = ends[1].astype(jnp.float32).reshape(groups, per_step, SEQ, D)
    route_blocks = jnp.transpose(routes.reshape(2, count, SEQ), (1, 0, 2)).reshape(groups, per_step, 2, SEQ)
    slot_blocks = jnp.transpose(slots.reshape(2, count, SEQ), (1, 0, 2)).reshape(groups, per_step, 2, SEQ)
    segment_blocks = segments.reshape(groups, per_step, SEQ)

    def forward(weights, inputs):

        def group(pieces):
            block_rows, route_pair, slot_pair, segment = pieces

            def single(one_rows, one_routes, one_slots, one_segment):
                return two_layers(weights, one_rows, one_routes, one_slots, one_segment, bucket_index)
            return jax.vmap(single)(block_rows, route_pair, slot_pair, segment)
        return lax.map(jax.checkpoint(group), (inputs, route_blocks, slot_blocks, segment_blocks))
    final, pull = jax.vjp(forward, weights, inputs)
    weight_grads, input_grad = pull(cotangent)
    ends_out = jnp.stack([input_grad.reshape(TOKENS, D), final.reshape(TOKENS, D)]).astype(jnp.bfloat16)
    return (ends_out, weight_grads[0], weight_grads[1], weight_grads[2], weight_grads[3], weight_grads[4], weight_grads[5], weight_grads[6], weight_grads[7], weight_grads[8], weight_grads[9])
```

```python
import jax
import jax.numpy as jnp
from jax import lax
from jax.sharding import PartitionSpec as P

epsilon = 1e-06
highest = lax.Precision.HIGHEST


def from_behind(value, axis, steps):
    count = lax.axis_size(axis)
    first, last = (max(0, -steps), min(count, count - steps))
    return lax.ppermute(value, axis, [(source, source + steps) for source in range(first, last)])


def normalize(values, gain):
    return values * lax.rsqrt(jnp.mean(values * values, axis=-1, keepdims=True) + epsilon) * gain


def gelu_both(values):
    below = 0.5 * (1.0 + lax.erf(values * (0.5**0.5)))
    density = jnp.exp(-0.5 * values * values) * ((2.0 * jnp.pi) ** -0.5)
    return (values * below).astype(jnp.bfloat16), (below + values * density).astype(jnp.bfloat16)


def spread_offsets(table_rows, length):
    heads = table_rows.shape[0]
    widened = jnp.broadcast_to(table_rows[:, None, :], (heads, length, 2 * length - 1)).reshape(
        heads, length * (2 * length - 1)
    )
    widened = jnp.concatenate([widened, jnp.zeros((heads, length), table_rows.dtype)], 1).reshape(
        heads, length, 2 * length
    )
    return widened[:, :, :length][:, :, ::-1]


def offset_sums(grads, length):
    heads = grads.shape[0]
    flipped = grads[:, :, ::-1]
    padded = jnp.concatenate([flipped, jnp.zeros((heads, length, length), grads.dtype)], 2).reshape(
        heads, 2 * length * length
    )
    return padded[:, : length * (2 * length - 1)].reshape(heads, length, 2 * length - 1).sum(1)


def shards(
    ends,
    w_query,
    w_key,
    w_value,
    w_output,
    gain_attention,
    gain_experts,
    router,
    bias_table,
    experts_up,
    experts_down,
    routes,
    slots,
    segments,
    buckets,
):
    section = lax.axis_index("section")
    first = section == 0
    length = (buckets.shape[0] + 1) // 2
    model = ends.shape[2]
    batches = ends.shape[1] // length
    owners = lax.axis_size("expert")
    layers = lax.axis_size("dp")
    mine = lax.axis_index("expert")
    projections = jnp.concatenate([w_query[0], w_key[0], w_value[0], w_output[0]], 1)
    piece = projections.shape[0] // owners
    small = jnp.concatenate(
        [
            gain_attention.reshape(1, -1),
            gain_experts.reshape(1, -1),
            router.reshape(1, -1),
            bias_table.reshape(1, -1),
        ],
        1,
    )
    gathered = lax.all_gather(
        lax.dynamic_slice_in_dim(projections, mine * piece, piece, 0),
        ("dp", "expert"),
        axis=0,
        tiled=True,
    )
    qkv_w = gathered[:, : 3 * model]
    output_w = gathered[:, 3 * model :]
    small = lax.all_gather(small, "dp", axis=0, tiled=True)
    rows = w_query.shape[1]
    kinds = router.shape[2]
    gain_one = small[:, :rows].reshape(-1).astype(jnp.float32)
    gain_two = small[:, rows : 2 * rows].reshape(-1).astype(jnp.float32)
    router_w = small[:, 2 * rows : (2 + kinds) * rows].reshape(-1, kinds)
    table = small[:, (2 + kinds) * rows :].reshape(-1, bias_table.shape[2]).astype(jnp.float32)
    up_w = lax.all_gather(experts_up, "dp", axis=2, tiled=True)[0]
    down_w = lax.all_gather(
        jnp.swapaxes(experts_down[0], 1, 2), "dp", axis=1, tiled=True
    )
    local = up_w.shape[0]
    experts = owners * local
    capacity = 2 * length // experts
    heads = table.shape[1]
    width = model // heads
    scale = width ** (-0.5)
    bucket_hot = (buckets[None, :] == jnp.arange(table.shape[0], dtype=jnp.int32)[:, None]).astype(
        jnp.float32
    )
    relative = spread_offsets(jnp.dot(table.T, bucket_hot, precision=highest), length)
    my_routes = routes[0].reshape(batches, length)
    my_slots = slots[0].reshape(batches, length)
    my_segments = segments.reshape(batches, length)
    data = ends[0].reshape(batches, length, model)
    expert_ids = jnp.arange(experts, dtype=jnp.int32)

    def attention_scores(queries, keys, segment):
        same = segment[:, None] == segment[None, :]
        scores = (
            jnp.einsum("qhd,khd->hqk", queries, keys, preferred_element_type=jnp.float32) * scale
            + relative
        )
        return jnp.where(same[None], scores, -1e30)

    def merged(all_steps):
        ends_step = jax.tree.map(pick, all_steps[batches], all_steps[0])
        return all_steps[1:batches] + [ends_step]

    def product_sum(parts, left, right, form):
        return sum(
            jnp.einsum(form, part[left], part[right], preferred_element_type=jnp.float32)
            for part in parts
        ).astype(jnp.bfloat16)

    def expert_sums(all_steps):
        names = ("arrived", "activated", "arrived_grad", "before_grad")
        parts = merged([{name: each[name] for name in names} for each in all_steps])
        return (
            product_sum(parts, "arrived", "before_grad", "secd,secf->edf"),
            product_sum(parts, "arrived_grad", "activated", "secd,secf->edf"),
        )

    received = jnp.zeros((length, model), jnp.bfloat16)
    stash = []
    produced = []
    for tick in range(batches + 1):
        early = min(tick, batches - 1)
        late = max(tick - 1, 0)
        inputs = jnp.where(first, data[early], received)
        route = jnp.where(first, my_routes[early], my_routes[late])
        slot = jnp.where(first, my_slots[early], my_slots[late])
        segment = jnp.where(first, my_segments[early], my_segments[late])
        current = inputs.astype(jnp.float32)
        forward_normed = normalize(current, gain_one).astype(jnp.bfloat16)
        projected = jnp.dot(forward_normed, qkv_w, preferred_element_type=jnp.float32).astype(
            jnp.bfloat16
        )
        forward_queries = projected[:, :model]
        forward_keys = projected[:, model : 2 * model]
        forward_values = projected[:, 2 * model :]
        forward_scores = attention_scores(
            forward_queries.reshape(length, heads, width),
            forward_keys.reshape(length, heads, width),
            segment,
        )
        peak = jnp.max(forward_scores, axis=-1, keepdims=True)
        raised = jnp.exp(forward_scores - peak)
        total = jnp.sum(raised, axis=-1, keepdims=True)
        forward_probs = raised / total
        log_total = peak + jnp.log(total)
        mixed = jnp.einsum(
            "hqk,khd->qhd",
            forward_probs.astype(jnp.bfloat16),
            forward_values.reshape(length, heads, width),
            preferred_element_type=jnp.float32,
        )
        mixed = mixed.reshape(length, model).astype(jnp.bfloat16)
        hidden = current + jnp.dot(mixed, output_w, preferred_element_type=jnp.float32)
        routed = normalize(hidden, gain_two).astype(jnp.bfloat16)
        chances = jax.nn.softmax(
            jnp.dot(routed, router_w, preferred_element_type=jnp.float32), axis=-1
        )
        forward_choose = (route[:, None] == expert_ids[None, :]).astype(jnp.float32)
        gate = jnp.sum(chances * forward_choose, axis=-1)
        target = route * capacity + slot
        spots = jnp.arange(experts * capacity, dtype=jnp.int32)
        place = (target[None, :] == spots[:, None]).astype(jnp.bfloat16)
        forward_outgoing = (
            jnp.dot(place, routed, preferred_element_type=jnp.float32)
            .astype(jnp.bfloat16)
            .reshape(owners, local * capacity, model)
        )
        arrived = lax.all_to_all(
            forward_outgoing, "expert", split_axis=0, concat_axis=0, tiled=True
        ).reshape(owners, local, capacity, model)
        before = jnp.einsum("secd,edf->secf", arrived, up_w, preferred_element_type=jnp.float32)
        activated, slope = gelu_both(before)
        activated, slope = lax.optimization_barrier((activated, slope))
        after = jnp.einsum(
            "secf,edf->secd", activated, down_w, preferred_element_type=jnp.float32
        ).astype(jnp.bfloat16)
        returned = lax.all_to_all(
            after.reshape(owners, local * capacity, model),
            "expert",
            split_axis=0,
            concat_axis=0,
            tiled=True,
        ).reshape(experts * capacity, model)
        forward_fetched = jnp.einsum(
            "sl,sd->ld", place, returned, preferred_element_type=jnp.float32
        ).astype(jnp.bfloat16)
        output = hidden + gate[:, None] * forward_fetched.astype(jnp.float32)
        forward_kept = {
            "inputs": inputs,
            "normed": forward_normed,
            "queries": forward_queries,
            "keys": forward_keys,
            "values": forward_values,
            "log_total": log_total,
            "mixed": mixed,
            "hidden": hidden,
            "routed": routed,
            "chances": chances,
            "gate": gate,
            "route": route,
            "place": place,
            "segment": segment,
            "arrived": arrived,
            "activated": activated,
            "slope": slope,
            "fetched": forward_fetched,
        }
        output, kept = (output, forward_kept)
        stash.append(kept)
        produced.append(output.astype(jnp.bfloat16))
        if tick < batches:
            received = from_behind(produced[-1], "section", 1)
    def pick(earlier, later):
        return earlier if earlier is later else jnp.where(first, earlier, later)

    steps = []
    arriving = jnp.zeros((length, model), jnp.bfloat16)
    results = []
    for tick in range(batches + 1):
        own = data[min(tick, batches - 1)]
        incoming = jnp.where(first, arriving, own).astype(jnp.float32)
        kept = jax.tree.map(pick, stash[max(tick - 1, 0)], stash[min(tick + 1, batches)])
        if tick == 0:
            kept = stash[min(1, batches)]
        elif tick == batches:
            kept = stash[batches - 1]
        grad_out = incoming
        fetched = kept["fetched"].astype(jnp.float32)
        gate_grad = jnp.sum(grad_out * fetched, axis=-1)
        weighted = (kept["gate"][:, None] * grad_out).astype(jnp.bfloat16)
        outgoing = (
            jnp.dot(kept["place"], weighted, preferred_element_type=jnp.float32)
            .astype(jnp.bfloat16)
            .reshape(owners, local * capacity, model)
        )
        arrived_grad = lax.all_to_all(
            outgoing, "expert", split_axis=0, concat_axis=0, tiled=True
        ).reshape(owners, local, capacity, model)
        activation_grad = jnp.einsum(
            "secd,edf->secf", arrived_grad, down_w, preferred_element_type=jnp.float32
        )
        before_grad = (activation_grad * kept["slope"].astype(jnp.float32)).astype(jnp.bfloat16)
        step = {
            "arrived": kept["arrived"],
            "activated": kept["activated"],
            "arrived_grad": arrived_grad,
            "before_grad": before_grad,
        }
        if tick == batches:
            steps.append(step)
            up_sum, down_sum = expert_sums(steps)
            up_sum, down_sum, before_grad = lax.optimization_barrier(
                (up_sum, down_sum, before_grad)
            )
            up_share = lax.psum_scatter(up_sum, "dp", scatter_dimension=1, tiled=True)
            down_share = lax.psum_scatter(down_sum, "dp", scatter_dimension=1, tiled=True)
        input_rows_grad = jnp.einsum(
            "secf,edf->secd", before_grad, up_w, preferred_element_type=jnp.float32
        ).astype(jnp.bfloat16)
        back_grad = lax.all_to_all(
            input_rows_grad.reshape(owners, local * capacity, model),
            "expert",
            split_axis=0,
            concat_axis=0,
            tiled=True,
        ).reshape(experts * capacity, model)
        routed_grad = jnp.einsum(
            "sl,sd->ld", kept["place"], back_grad, preferred_element_type=jnp.float32
        )
        choose = (kept["route"][:, None] == expert_ids[None, :]).astype(jnp.float32)
        logit_grad = kept["chances"] * (
            gate_grad[:, None] * choose - (gate_grad * kept["gate"])[:, None]
        )
        routed_full = kept["routed"].astype(jnp.float32)
        router_part = jnp.dot(routed_full.T, logit_grad, precision=highest)
        routed_grad = routed_grad + jnp.dot(
            logit_grad, router_w.astype(jnp.float32).T, precision=highest
        )
        second_pull = jax.vjp(normalize, kept["hidden"], gain_two)[1]
        hidden_part, gain_two_part = second_pull(routed_grad)
        hidden_grad = grad_out + hidden_part
        branch_grad = hidden_grad.astype(jnp.bfloat16)
        mixed_grad = (
            jnp.einsum("le,ce->lc", branch_grad, output_w, preferred_element_type=jnp.float32)
            .astype(jnp.bfloat16)
            .reshape(length, heads, width)
        )
        backward_queries = kept["queries"].reshape(length, heads, width)
        backward_keys = kept["keys"].reshape(length, heads, width)
        values = kept["values"].reshape(length, heads, width)
        probs = jnp.exp(
            attention_scores(backward_queries, backward_keys, kept["segment"]) - kept["log_total"]
        )
        prob_grad = jnp.einsum(
            "qhd,khd->hqk", mixed_grad, values, preferred_element_type=jnp.float32
        )
        value_grad = (
            jnp.einsum(
                "hqk,qhd->khd",
                probs.astype(jnp.bfloat16),
                mixed_grad,
                preferred_element_type=jnp.float32,
            )
            .astype(jnp.bfloat16)
            .reshape(length, model)
        )
        inner = jnp.sum(probs * prob_grad, axis=-1, keepdims=True)
        score_grad = (probs * (prob_grad - inner)).astype(jnp.bfloat16)
        query_grad = (
            (
                jnp.einsum(
                    "hqk,khd->qhd", score_grad, backward_keys, preferred_element_type=jnp.float32
                )
                * scale
            )
            .astype(jnp.bfloat16)
            .reshape(length, model)
        )
        key_grad = (
            (
                jnp.einsum(
                    "hqk,qhd->khd", score_grad, backward_queries, preferred_element_type=jnp.float32
                )
                * scale
            )
            .astype(jnp.bfloat16)
            .reshape(length, model)
        )
        projected_grad = jnp.concatenate([query_grad, key_grad, value_grad], 1)
        normed_grad = jnp.einsum(
            "le,ce->lc", projected_grad, qkv_w, preferred_element_type=jnp.float32
        )
        first_pull = jax.vjp(normalize, kept["inputs"].astype(jnp.float32), gain_one)[1]
        input_part, gain_one_part = first_pull(normed_grad)
        step["normed"] = kept["normed"]
        step["mixed"] = kept["mixed"]
        step["branch_grad"] = branch_grad
        step["projected_grad"] = projected_grad
        step["router"] = router_part
        step["gain_one"] = gain_one_part
        step["gain_two"] = gain_two_part
        step["score_grad"] = score_grad
        if tick < batches:
            steps.append(step)
        grad_in = hidden_grad + input_part
        results.append(grad_in.astype(jnp.bfloat16))
        if tick < batches:
            arriving = from_behind(results[-1], "section", -1)
    blocks = [jnp.where(first, results[index + 1], produced[index + 1]) for index in range(batches)]
    ends_out = jnp.concatenate(blocks, 0)[None]
    parts = merged(steps)
    score_sum = sum(part["score_grad"].astype(jnp.float32) for part in parts)
    table_sum = jnp.dot(bucket_hot, offset_sums(score_sum, length).T, precision=highest)
    projection_sum = jnp.concatenate(
        [
            product_sum(parts, "normed", "projected_grad", "lc,le->ce"),
            product_sum(parts, "mixed", "branch_grad", "lc,le->ce"),
        ],
        1,
    )
    shares = lax.all_gather(
        lax.psum_scatter(projection_sum, ("dp", "expert"), scatter_dimension=0, tiled=True),
        "expert",
        axis=0,
        tiled=True,
    ).astype(jnp.float32)
    small_sum = jnp.concatenate(
        [
            sum(part["gain_one"] for part in parts).reshape(layers, -1),
            sum(part["gain_two"] for part in parts).reshape(layers, -1),
            sum(part["router"] for part in parts).reshape(layers, -1),
            table_sum.reshape(layers, -1),
        ],
        1,
    ).astype(jnp.bfloat16)
    small_share = lax.dynamic_index_in_dim(
        lax.psum(small_sum, ("dp", "expert")), lax.axis_index("dp"), 0, keepdims=False
    ).astype(jnp.float32)
    return (
        ends_out,
        shares[None, :, :model],
        shares[None, :, model : 2 * model],
        shares[None, :, 2 * model : 3 * model],
        shares[None, :, 3 * model :],
        small_share[None, :rows],
        small_share[None, rows : 2 * rows],
        small_share[2 * rows : (2 + kinds) * rows].reshape(1, rows, kinds),
        small_share[(2 + kinds) * rows :].reshape(1, -1, bias_table.shape[2]),
        up_share.astype(jnp.float32)[None],
        jnp.swapaxes(down_share.astype(jnp.float32), 1, 2)[None],
    )


def solution(mesh):
    in_specs = (
        P("section", ("dp", "expert"), None),
        P("section", "dp", None),
        P("section", "dp", None),
        P("section", "dp", None),
        P("section", "dp", None),
        P("section", "dp"),
        P("section", "dp"),
        P("section", "dp", None),
        P("section", "dp", None),
        P("section", "expert", "dp", None),
        P("section", "expert", None, "dp"),
        P("section", ("dp", "expert")),
        P("section", ("dp", "expert")),
        P(("dp", "expert")),
        P(),
    )
    out_specs = (
        P("section", ("dp", "expert"), None),
        P("section", "dp", None),
        P("section", "dp", None),
        P("section", "dp", None),
        P("section", "dp", None),
        P("section", "dp"),
        P("section", "dp"),
        P("section", "dp", None),
        P("section", "dp", None),
        P("section", "expert", "dp", None),
        P("section", "expert", None, "dp"),
    )
    return jax.shard_map(shards, mesh=mesh, in_specs=in_specs, out_specs=out_specs, check_vma=False)
```

```python
import functools
from typing import NamedTuple

import jax
import jax.numpy as jnp
from jax import lax
from jax.experimental import pallas as pl
from jax.experimental.pallas import tpu as pltpu
from jax.sharding import PartitionSpec as P

SECTION, DP, EXPERT = "section", "dp", "expert"
epsilon = 1e-06
highest = lax.Precision.HIGHEST


class Kept(NamedTuple):
    inputs: jax.Array
    normed: jax.Array
    projected: jax.Array
    mixed: jax.Array
    hidden: jax.Array
    routed: jax.Array
    chances: jax.Array
    gate: jax.Array
    route: jax.Array
    place: jax.Array
    segment: jax.Array
    arrived: jax.Array
    activated: jax.Array
    slope: jax.Array
    fetched: jax.Array


class ExpertStep(NamedTuple):
    arrived: jax.Array
    activated: jax.Array
    arrived_grad: jax.Array
    before_grad: jax.Array


class SharedStep(NamedTuple):
    normed: jax.Array
    mixed: jax.Array
    branch_grad: jax.Array
    projected_grad: jax.Array
    router: jax.Array
    gain_one: jax.Array
    gain_two: jax.Array
    score_grad: jax.Array


def from_behind(value, axis, steps):
    count = lax.axis_size(axis)
    first, last = (max(0, -steps), min(count, count - steps))
    return lax.ppermute(value, axis, [(source, source + steps) for source in range(first, last)])


def normalize(values, gain):
    return values * lax.rsqrt(jnp.mean(values * values, axis=-1, keepdims=True) + epsilon) * gain


def gelu_both(values):
    below = 0.5 * (1.0 + lax.erf(values * (0.5**0.5)))
    density = jnp.exp(-0.5 * values * values) * ((2.0 * jnp.pi) ** -0.5)
    return (values * below).astype(jnp.bfloat16), (below + values * density).astype(jnp.bfloat16)


def head_scores(query, key, bias, same):
    scores = lax.dot_general(
        query, key, (((1,), (1,)), ((), ())), preferred_element_type=jnp.float32
    )
    scores = jnp.where(same, scores * (query.shape[1] ** -0.5) + bias, -1e30)
    raised = jnp.exp(scores - jnp.max(scores, axis=-1, keepdims=True))
    return raised / jnp.sum(raised, axis=-1, keepdims=True)


def forward_body(width, column, row, query, key, value, bias, mixed):
    same = column[...] == row[...]
    parts = []
    for head in range(bias.shape[0]):
        lanes = slice(head * width, (head + 1) * width)
        probs = head_scores(query[:, lanes], key[:, lanes], bias[head], same)
        parts.append(
            jnp.dot(
                probs.astype(jnp.bfloat16), value[:, lanes], preferred_element_type=jnp.float32
            )
        )
    mixed[...] = jnp.concatenate(parts, 1).astype(jnp.bfloat16)


def backward_body(
    width, column, row, query, key, value, mixed, bias, query_out, key_out, value_out, score_out
):
    same = column[...] == row[...]
    scale = width**-0.5
    rows = (((0,), (0,)), ((), ()))
    columns = (((1,), (1,)), ((), ()))
    query_parts, key_parts, value_parts = [], [], []
    for head in range(bias.shape[0]):
        lanes = slice(head * width, (head + 1) * width)
        own_query, own_key, grad = query[:, lanes], key[:, lanes], mixed[:, lanes]
        probs = head_scores(own_query, own_key, bias[head], same)
        prob_grad = lax.dot_general(
            grad, value[:, lanes], columns, preferred_element_type=jnp.float32
        )
        value_parts.append(
            lax.dot_general(
                probs.astype(jnp.bfloat16), grad, rows, preferred_element_type=jnp.float32
            )
        )
        inner = jnp.sum(probs * prob_grad, axis=-1, keepdims=True)
        score_grad = (probs * (prob_grad - inner)).astype(jnp.bfloat16)
        score_out[head] = score_grad
        query_parts.append(jnp.dot(score_grad, own_key, preferred_element_type=jnp.float32))
        key_parts.append(
            lax.dot_general(score_grad, own_query, rows, preferred_element_type=jnp.float32)
        )
    query_out[...] = (jnp.concatenate(query_parts, 1) * scale).astype(jnp.bfloat16)
    key_out[...] = (jnp.concatenate(key_parts, 1) * scale).astype(jnp.bfloat16)
    value_out[...] = jnp.concatenate(value_parts, 1).astype(jnp.bfloat16)


def spread_body(rows, relative):
    length = relative.shape[1]
    wide = jnp.broadcast_to(rows[0], (length, 2 * length))
    relative[0] = pltpu.roll(wide, 0, 1, stride=1, stride_axis=0)[:, :length]


def offset_body(one, two, sums):
    length = one.shape[1]
    down = lax.broadcasted_iota(jnp.int32, (length, length), 0)
    across = lax.broadcasted_iota(jnp.int32, (length, length), 1)
    turn = (down + across == length - 1).astype(jnp.bfloat16)
    turned = jnp.dot(one[0], turn, preferred_element_type=jnp.float32) + jnp.dot(
        two[0], turn, preferred_element_type=jnp.float32
    )
    wide = jnp.concatenate([turned, jnp.zeros((length, length), jnp.float32)], 1)
    sums[0] = jnp.sum(
        pltpu.roll(wide, 0, 1, stride=1, stride_axis=0), axis=0, keepdims=True
    )


def attention_specs(length, heads, width):
    group = 2 if heads % 2 == 0 else heads
    groups = heads // group
    line = pl.BlockSpec((length, 1), lambda step: (0, 0))
    flat = pl.BlockSpec((1, length), lambda step: (0, 0))
    blocks = [
        pl.BlockSpec((length, group * width), lambda step, shift=shift: (0, step + shift * groups))
        for shift in range(3)
    ]
    square = pl.BlockSpec((group, length, length), lambda step: (step, 0, 0))
    return groups, line, flat, blocks, square


roomy = 40 * 1024 * 1024


def attend(projected, relative, segment):
    heads, length, _ = relative.shape
    model = projected.shape[1] // 3
    groups, line, flat, blocks, square = attention_specs(length, heads, model // heads)
    return pl.pallas_call(
        functools.partial(forward_body, model // heads),
        grid=(groups,),
        in_specs=[line, flat, *blocks, square],
        out_specs=blocks[0],
        out_shape=jax.ShapeDtypeStruct((length, model), jnp.bfloat16),
        compiler_params=pltpu.CompilerParams(vmem_limit_bytes=roomy),
        name="attend",
    )(segment[:, None], segment[None, :], projected, projected, projected, relative)


def attend_back(projected, mixed_grad, relative, segment):
    heads, length, _ = relative.shape
    model = projected.shape[1] // 3
    groups, line, flat, blocks, square = attention_specs(length, heads, model // heads)
    piece = jax.ShapeDtypeStruct((length, model), jnp.bfloat16)
    return pl.pallas_call(
        functools.partial(backward_body, model // heads),
        grid=(groups,),
        in_specs=[line, flat, *blocks, blocks[0], square],
        out_specs=[blocks[0], blocks[0], blocks[0], square],
        out_shape=[piece, piece, piece, jax.ShapeDtypeStruct(relative.shape, jnp.bfloat16)],
        compiler_params=pltpu.CompilerParams(vmem_limit_bytes=roomy),
        name="attend_back",
    )(segment[:, None], segment[None, :], projected, projected, projected, mixed_grad, relative)


def spread_offsets(rows, length):
    heads = rows.shape[0]
    return pl.pallas_call(
        spread_body,
        grid=(heads,),
        in_specs=[pl.BlockSpec((1, 1, 2 * length), lambda head: (head, 0, 0))],
        out_specs=pl.BlockSpec((1, length, length), lambda head: (head, 0, 0)),
        out_shape=jax.ShapeDtypeStruct((heads, length, length), jnp.float32),
        name="spread_offsets",
    )(rows[:, None, :])


def offset_sums(one, two):
    heads, length, _ = one.shape
    square = pl.BlockSpec((1, length, length), lambda head: (head, 0, 0))
    return pl.pallas_call(
        offset_body,
        grid=(heads,),
        in_specs=[square, square],
        out_specs=pl.BlockSpec((1, 1, 2 * length), lambda head: (head, 0, 0)),
        out_shape=jax.ShapeDtypeStruct((heads, 1, 2 * length), jnp.float32),
        name="offset_sums",
    )(one, two)[:, 0, : 2 * length - 1]


def shards(
    ends,
    w_query,
    w_key,
    w_value,
    w_output,
    gain_attention,
    gain_experts,
    router,
    bias_table,
    experts_up,
    experts_down,
    routes,
    slots,
    segments,
    buckets,
):
    section = lax.axis_index(SECTION)
    first = section == 0
    length = (buckets.shape[0] + 1) // 2
    model = ends.shape[2]
    batches = ends.shape[1] // length
    owners = lax.axis_size(EXPERT)
    layers = lax.axis_size(DP)
    mine = lax.axis_index(EXPERT)
    projections = jnp.concatenate([w_query[0], w_key[0], w_value[0], w_output[0]], 1)
    piece = projections.shape[0] // owners
    small = jnp.concatenate(
        [
            gain_attention.reshape(1, -1),
            gain_experts.reshape(1, -1),
            router.reshape(1, -1),
            bias_table.reshape(1, -1),
        ],
        1,
    )
    quarter = lax.all_gather(
        lax.dynamic_slice_in_dim(projections, mine * piece, piece, 0), DP, axis=0
    )

    def spread(block):
        return lax.all_to_all(
            jnp.broadcast_to(block[None], (owners, *block.shape)),
            EXPERT,
            split_axis=0,
            concat_axis=0,
            tiled=True,
        )

    small = lax.all_gather(small, DP, axis=0, tiled=True)
    rows = w_query.shape[1]
    kinds = router.shape[2]
    gain_one = small[:, :rows].reshape(-1).astype(jnp.float32)
    gain_two = small[:, rows : 2 * rows].reshape(-1).astype(jnp.float32)
    router_w = small[:, 2 * rows : (2 + kinds) * rows].reshape(-1, kinds)
    table = small[:, (2 + kinds) * rows :].reshape(-1, bias_table.shape[2]).astype(jnp.float32)
    own_up = experts_up[0]
    own_down = jnp.swapaxes(experts_down[0], 1, 2)
    swapped = lax.ppermute(jnp.where(first, own_down, own_up), SECTION, [(0, 1), (1, 0)])
    own_up, own_down, swapped, quarter = lax.optimization_barrier(
        (own_up, own_down, swapped, quarter)
    )
    early_w = lax.all_gather(jnp.where(first, own_up, swapped), DP, axis=1, tiled=True)
    late_w = lax.all_gather(jnp.where(first, swapped, own_down), DP, axis=1, tiled=True)
    early_down = lax.ppermute(early_w, SECTION, [(1, 0)])
    late_up = lax.ppermute(late_w, SECTION, [(0, 1)])
    up_w = jnp.where(first, early_w, late_up)
    down_w = jnp.where(first, early_down, late_w)
    gathered = jnp.swapaxes(spread(quarter), 0, 1).reshape(layers * owners * piece, -1)
    qkv_w = gathered[:, : 3 * model]
    output_w = gathered[:, 3 * model :]
    local = up_w.shape[0]
    experts = owners * local
    capacity = 2 * length // experts
    heads = table.shape[1]
    bucket_hot = (buckets[None, :] == jnp.arange(table.shape[0], dtype=jnp.int32)[:, None]).astype(
        jnp.float32
    )
    backwards = jnp.concatenate(
        [buckets[:length][::-1], jnp.full((1,), -1, jnp.int32), buckets[length:][::-1]]
    )
    backwards_hot = (
        backwards[None, :] == jnp.arange(table.shape[0], dtype=jnp.int32)[:, None]
    ).astype(jnp.float32)
    relative = spread_offsets(jnp.dot(table.T, backwards_hot, precision=highest), length)
    my_routes = routes[0].reshape(batches, length)
    my_slots = slots[0].reshape(batches, length)
    my_segments = segments.reshape(batches, length)
    data = ends[0].reshape(batches, length, model)
    expert_ids = jnp.arange(experts, dtype=jnp.int32)

    def merged(all_steps):
        ends_step = jax.tree.map(pick, all_steps[batches], all_steps[0])
        return all_steps[1:batches] + [ends_step]

    def product(lefts, rights):
        return lax.dot_general(
            jnp.concatenate(lefts, 0),
            jnp.concatenate(rights, 0),
            (((0,), (0,)), ((), ())),
            preferred_element_type=jnp.float32,
        ).astype(jnp.bfloat16)

    def expert_product(lefts, rights):
        return jnp.stack(
            [
                product(
                    [left[:, one].reshape(-1, left.shape[3]) for left in lefts],
                    [right[:, one].reshape(-1, right.shape[3]) for right in rights],
                )
                for one in range(local)
            ]
        )

    def later_sums(*all_steps):
        return (
            expert_product(
                [each.arrived for each in all_steps], [each.before_grad for each in all_steps]
            ),
            expert_product(
                [each.arrived_grad for each in all_steps], [each.activated for each in all_steps]
            ),
        )

    def empty_sums(*all_steps):
        shape = up_w.shape
        return jnp.zeros(shape, jnp.bfloat16), jnp.zeros(shape, jnp.bfloat16)

    received = jnp.zeros((length, model), jnp.bfloat16)
    stash = []
    produced = []
    for tick in range(batches + 1):
        early = min(tick, batches - 1)
        late = max(tick - 1, 0)
        inputs = jnp.where(first, data[early], received)
        route = jnp.where(first, my_routes[early], my_routes[late])
        slot = jnp.where(first, my_slots[early], my_slots[late])
        segment = jnp.where(first, my_segments[early], my_segments[late])
        current = inputs.astype(jnp.float32)
        forward_normed = normalize(current, gain_one).astype(jnp.bfloat16)
        projected = jnp.dot(forward_normed, qkv_w, preferred_element_type=jnp.float32).astype(
            jnp.bfloat16
        )
        mixed = attend(projected, relative, segment)
        hidden = current + jnp.dot(mixed, output_w, preferred_element_type=jnp.float32)
        routed = normalize(hidden, gain_two).astype(jnp.bfloat16)
        chances = jax.nn.softmax(
            jnp.dot(routed, router_w, preferred_element_type=jnp.float32), axis=-1
        )
        forward_choose = (route[:, None] == expert_ids[None, :]).astype(jnp.float32)
        gate = jnp.sum(chances * forward_choose, axis=-1)
        target = route * capacity + slot
        spots = jnp.arange(experts * capacity, dtype=jnp.int32)
        place = (target[None, :] == spots[:, None]).astype(jnp.bfloat16)
        forward_outgoing = (
            jnp.dot(place, routed, preferred_element_type=jnp.float32)
            .astype(jnp.bfloat16)
            .reshape(owners, local * capacity, model)
        )
        arrived = lax.all_to_all(
            forward_outgoing, EXPERT, split_axis=0, concat_axis=0, tiled=True
        ).reshape(owners, local, capacity, model)
        tick_up, tick_down = (early_w, early_down) if tick == 0 else (up_w, down_w)
        before = jnp.einsum("secd,edf->secf", arrived, tick_up, preferred_element_type=jnp.float32)
        activated, slope = gelu_both(before)
        activated, slope = lax.optimization_barrier((activated, slope))
        after = jnp.einsum(
            "secf,edf->secd", activated, tick_down, preferred_element_type=jnp.float32
        ).astype(jnp.bfloat16)
        returned = lax.all_to_all(
            after.reshape(owners, local * capacity, model),
            EXPERT,
            split_axis=0,
            concat_axis=0,
            tiled=True,
        ).reshape(experts * capacity, model)
        forward_fetched = jnp.einsum(
            "sl,sd->ld", place, returned, preferred_element_type=jnp.float32
        ).astype(jnp.bfloat16)
        output = hidden + gate[:, None] * forward_fetched.astype(jnp.float32)
        forward_kept = Kept(
            inputs=inputs,
            normed=forward_normed,
            projected=projected,
            mixed=mixed,
            hidden=hidden,
            routed=routed,
            chances=chances,
            gate=gate,
            route=route,
            place=place,
            segment=segment,
            arrived=arrived,
            activated=activated,
            slope=slope,
            fetched=forward_fetched,
        )
        output, kept = (output, forward_kept)
        stash.append(kept)
        produced.append(output.astype(jnp.bfloat16))
        if tick < batches:
            received = from_behind(produced[-1], SECTION, 1)
    def pick(earlier, later):
        return earlier if earlier is later else jnp.where(first, earlier, later)

    steps = []
    expert_steps = []
    arriving = jnp.zeros((length, model), jnp.bfloat16)
    results = []
    for tick in range(batches + 1):
        own = data[min(tick, batches - 1)]
        incoming = jnp.where(first, arriving, own).astype(jnp.float32)
        kept = jax.tree.map(pick, stash[max(tick - 1, 0)], stash[min(tick + 1, batches)])
        if tick == 0:
            kept = stash[min(1, batches)]
        elif tick == batches:
            kept = stash[batches - 1]
        grad_out = incoming
        fetched = kept.fetched.astype(jnp.float32)
        gate_grad = jnp.sum(grad_out * fetched, axis=-1)
        weighted = (kept.gate[:, None] * grad_out).astype(jnp.bfloat16)
        outgoing = (
            jnp.dot(kept.place, weighted, preferred_element_type=jnp.float32)
            .astype(jnp.bfloat16)
            .reshape(owners, local * capacity, model)
        )
        arrived_grad = lax.all_to_all(
            outgoing, EXPERT, split_axis=0, concat_axis=0, tiled=True
        ).reshape(owners, local, capacity, model)
        activation_grad = jnp.einsum(
            "secd,edf->secf", arrived_grad, down_w, preferred_element_type=jnp.float32
        )
        before_grad = (activation_grad * kept.slope.astype(jnp.float32)).astype(jnp.bfloat16)
        expert_steps.append(ExpertStep(kept.arrived, kept.activated, arrived_grad, before_grad))
        if tick == batches:
            expert_sums = lax.cond(first, later_sums, empty_sums, *expert_steps[1:])
            kept_sums, before_grad = lax.optimization_barrier((expert_sums, before_grad))
            up_sum, down_sum = kept_sums
            swapped = lax.ppermute(down_sum, SECTION, [(0, 1)])
            late_share = lax.psum_scatter(
                jnp.where(first, up_sum, swapped), DP, scatter_dimension=1, tiled=True
            )
        input_rows_grad = jnp.einsum(
            "secf,edf->secd", before_grad, up_w, preferred_element_type=jnp.float32
        ).astype(jnp.bfloat16)
        back_grad = lax.all_to_all(
            input_rows_grad.reshape(owners, local * capacity, model),
            EXPERT,
            split_axis=0,
            concat_axis=0,
            tiled=True,
        ).reshape(experts * capacity, model)
        routed_grad = jnp.einsum(
            "sl,sd->ld", kept.place, back_grad, preferred_element_type=jnp.float32
        )
        choose = (kept.route[:, None] == expert_ids[None, :]).astype(jnp.float32)
        logit_grad = kept.chances * (
            gate_grad[:, None] * choose - (gate_grad * kept.gate)[:, None]
        )
        routed_full = kept.routed.astype(jnp.float32)
        router_part = jnp.dot(routed_full.T, logit_grad, precision=highest)
        routed_grad = routed_grad + jnp.dot(
            logit_grad, router_w.astype(jnp.float32).T, precision=highest
        )
        second_pull = jax.vjp(normalize, kept.hidden, gain_two)[1]
        hidden_part, gain_two_part = second_pull(routed_grad)
        hidden_grad = grad_out + hidden_part
        branch_grad = hidden_grad.astype(jnp.bfloat16)
        mixed_grad = jnp.einsum(
            "le,ce->lc", branch_grad, output_w, preferred_element_type=jnp.float32
        ).astype(jnp.bfloat16)
        *projected_grad, score_grad = attend_back(
            kept.projected, mixed_grad, relative, kept.segment
        )
        projected_grad = jnp.concatenate(projected_grad, 1)
        normed_grad = jnp.einsum(
            "le,ce->lc", projected_grad, qkv_w, preferred_element_type=jnp.float32
        )
        first_pull = jax.vjp(normalize, kept.inputs.astype(jnp.float32), gain_one)[1]
        input_part, gain_one_part = first_pull(normed_grad)
        steps.append(
            SharedStep(
                kept.normed,
                kept.mixed,
                branch_grad,
                projected_grad,
                router_part,
                gain_one_part,
                gain_two_part,
                score_grad,
            )
        )
        grad_in = hidden_grad + input_part
        results.append(grad_in.astype(jnp.bfloat16))
        if tick < batches:
            arriving = from_behind(results[-1], SECTION, -1)
        if tick == batches - 1:
            up_sum, down_sum = lax.cond(first, empty_sums, later_sums, *expert_steps)
            swapped = lax.ppermute(up_sum, SECTION, [(1, 0)])
            early_share = lax.psum_scatter(
                jnp.where(first, swapped, down_sum), DP, scatter_dimension=1, tiled=True
            )
    blocks = [jnp.where(first, results[index + 1], produced[index + 1]) for index in range(batches)]
    ends_out = jnp.concatenate(blocks, 0)[None]
    parts = merged(steps)
    score_pairs = [part.score_grad for part in parts]
    offsets = offset_sums(score_pairs[0], score_pairs[1])
    table_sum = jnp.dot(bucket_hot, offsets.T, precision=highest)
    projection_sum = jnp.concatenate(
        [
            product([part.normed for part in parts], [part.projected_grad for part in parts]),
            product([part.mixed for part in parts], [part.branch_grad for part in parts]),
        ],
        1,
    ).reshape(layers, owners, piece, 4 * model)
    quarters = lax.all_to_all(projection_sum, EXPERT, split_axis=1, concat_axis=1, tiled=True)
    quarter = quarters.astype(jnp.float32).sum(1).astype(jnp.bfloat16)
    share = lax.psum_scatter(
        quarter.reshape(layers * piece, 4 * model), DP, scatter_dimension=0, tiled=True
    )
    shares = spread(share).reshape(owners * piece, 4 * model).astype(jnp.float32)
    exchanged = lax.ppermute(
        jnp.where(first, early_share, late_share), SECTION, [(0, 1), (1, 0)]
    )
    up_share = jnp.where(first, late_share, exchanged).reshape(experts_up.shape)
    down_share = jnp.where(first, exchanged, early_share).reshape(local, -1, up_w.shape[2])
    small_sum = jnp.concatenate(
        [
            sum(part.gain_one for part in parts).reshape(layers, -1),
            sum(part.gain_two for part in parts).reshape(layers, -1),
            sum(part.router for part in parts).reshape(layers, -1),
            table_sum.reshape(layers, -1),
        ],
        1,
    ).astype(jnp.bfloat16)
    small_share = lax.dynamic_index_in_dim(
        lax.psum(small_sum, (DP, EXPERT)), lax.axis_index(DP), 0, keepdims=False
    ).astype(jnp.float32)
    return (
        ends_out,
        shares[None, :, :model],
        shares[None, :, model : 2 * model],
        shares[None, :, 2 * model : 3 * model],
        shares[None, :, 3 * model :],
        small_share[None, :rows],
        small_share[None, rows : 2 * rows],
        small_share[2 * rows : (2 + kinds) * rows].reshape(1, rows, kinds),
        small_share[(2 + kinds) * rows :].reshape(1, -1, bias_table.shape[2]),
        up_share.astype(jnp.float32),
        jnp.swapaxes(down_share.astype(jnp.float32), 1, 2)[None],
    )


def solution(mesh):
    in_specs = (
        P(SECTION, (DP, EXPERT), None),
        P(SECTION, DP, None),
        P(SECTION, DP, None),
        P(SECTION, DP, None),
        P(SECTION, DP, None),
        P(SECTION, DP),
        P(SECTION, DP),
        P(SECTION, DP, None),
        P(SECTION, DP, None),
        P(SECTION, EXPERT, DP, None),
        P(SECTION, EXPERT, None, DP),
        P(SECTION, (DP, EXPERT)),
        P(SECTION, (DP, EXPERT)),
        P((DP, EXPERT)),
        P(),
    )
    out_specs = (
        P(SECTION, (DP, EXPERT), None),
        P(SECTION, DP, None),
        P(SECTION, DP, None),
        P(SECTION, DP, None),
        P(SECTION, DP, None),
        P(SECTION, DP),
        P(SECTION, DP),
        P(SECTION, DP, None),
        P(SECTION, DP, None),
        P(SECTION, EXPERT, DP, None),
        P(SECTION, EXPERT, None, DP),
    )
    return jax.shard_map(shards, mesh=mesh, in_specs=in_specs, out_specs=out_specs, check_vma=False)
```

```python
import functools
from typing import NamedTuple

import jax
import jax.numpy as jnp
from jax import lax
from jax.experimental import pallas as pl
from jax.experimental.pallas import tpu as pltpu
from jax.sharding import PartitionSpec as P

SECTION, DP, EXPERT = "section", "dp", "expert"
epsilon = 1e-06
highest = lax.Precision.HIGHEST


class Kept(NamedTuple):
    inputs: jax.Array
    normed: jax.Array
    projected: jax.Array
    mixed: jax.Array
    hidden: jax.Array
    routed: jax.Array
    chances: jax.Array
    gate: jax.Array
    route: jax.Array
    place: jax.Array
    segment: jax.Array
    arrived: jax.Array
    activated: jax.Array
    slope: jax.Array
    fetched: jax.Array


class ExpertStep(NamedTuple):
    arrived: jax.Array
    activated: jax.Array
    arrived_grad: jax.Array
    before_grad: jax.Array


class SharedStep(NamedTuple):
    normed: jax.Array
    mixed: jax.Array
    branch_grad: jax.Array
    projected_grad: jax.Array
    router: jax.Array
    gain_one: jax.Array
    gain_two: jax.Array
    score_grad: jax.Array


def from_behind(value, axis, steps):
    count = lax.axis_size(axis)
    first, last = (max(0, -steps), min(count, count - steps))
    return lax.ppermute(value, axis, [(source, source + steps) for source in range(first, last)])


def normalize(values, gain):
    return values * lax.rsqrt(jnp.mean(values * values, axis=-1, keepdims=True) + epsilon) * gain


def gelu_both(values):
    below = 0.5 * (1.0 + lax.erf(values * (0.5**0.5)))
    density = jnp.exp(-0.5 * values * values) * ((2.0 * jnp.pi) ** -0.5)
    return (values * below).astype(jnp.bfloat16), (below + values * density).astype(jnp.bfloat16)


def head_scores(query, key, bias, same):
    scores = lax.dot_general(
        query, key, (((1,), (1,)), ((), ())), preferred_element_type=jnp.float32
    )
    scores = jnp.where(same, scores * (query.shape[1] ** -0.5) + bias, -1e30)
    raised = jnp.exp(scores - jnp.max(scores, axis=-1, keepdims=True))
    return raised / jnp.sum(raised, axis=-1, keepdims=True)


def forward_body(width, column, row, query, key, value, bias, mixed):
    same = column[...] == row[...]
    parts = []
    for head in range(bias.shape[0]):
        lanes = slice(head * width, (head + 1) * width)
        probs = head_scores(query[:, lanes], key[:, lanes], bias[head], same)
        parts.append(
            jnp.dot(
                probs.astype(jnp.bfloat16), value[:, lanes], preferred_element_type=jnp.float32
            )
        )
    mixed[...] = jnp.concatenate(parts, 1).astype(jnp.bfloat16)


def backward_body(
    width, column, row, query, key, value, mixed, bias, query_out, key_out, value_out, score_out
):
    same = column[...] == row[...]
    scale = width**-0.5
    rows = (((0,), (0,)), ((), ()))
    columns = (((1,), (1,)), ((), ()))
    query_parts, key_parts, value_parts = [], [], []
    for head in range(bias.shape[0]):
        lanes = slice(head * width, (head + 1) * width)
        own_query, own_key, grad = query[:, lanes], key[:, lanes], mixed[:, lanes]
        probs = head_scores(own_query, own_key, bias[head], same)
        prob_grad = lax.dot_general(
            grad, value[:, lanes], columns, preferred_element_type=jnp.float32
        )
        value_parts.append(
            lax.dot_general(
                probs.astype(jnp.bfloat16), grad, rows, preferred_element_type=jnp.float32
            )
        )
        inner = jnp.sum(probs * prob_grad, axis=-1, keepdims=True)
        score_grad = (probs * (prob_grad - inner)).astype(jnp.bfloat16)
        score_out[head] = score_grad
        query_parts.append(jnp.dot(score_grad, own_key, preferred_element_type=jnp.float32))
        key_parts.append(
            lax.dot_general(score_grad, own_query, rows, preferred_element_type=jnp.float32)
        )
    query_out[...] = (jnp.concatenate(query_parts, 1) * scale).astype(jnp.bfloat16)
    key_out[...] = (jnp.concatenate(key_parts, 1) * scale).astype(jnp.bfloat16)
    value_out[...] = jnp.concatenate(value_parts, 1).astype(jnp.bfloat16)


def spread_body(rows, relative):
    length = relative.shape[1]
    wide = jnp.broadcast_to(rows[0], (length, 2 * length))
    relative[0] = pltpu.roll(wide, 0, 1, stride=1, stride_axis=0)[:, :length]


def offset_body(one, two, sums):
    length = one.shape[1]
    down = lax.broadcasted_iota(jnp.int32, (length, length), 0)
    across = lax.broadcasted_iota(jnp.int32, (length, length), 1)
    turn = (down + across == length - 1).astype(jnp.bfloat16)
    turned = jnp.dot(one[0], turn, preferred_element_type=jnp.float32) + jnp.dot(
        two[0], turn, preferred_element_type=jnp.float32
    )
    wide = jnp.concatenate([turned, jnp.zeros((length, length), jnp.float32)], 1)
    sums[0] = jnp.sum(
        pltpu.roll(wide, 0, 1, stride=1, stride_axis=0), axis=0, keepdims=True
    )


def attention_specs(length, heads, width):
    group = 2 if heads % 2 == 0 else heads
    groups = heads // group
    line = pl.BlockSpec((length, 1), lambda step: (0, 0))
    flat = pl.BlockSpec((1, length), lambda step: (0, 0))
    blocks = [
        pl.BlockSpec((length, group * width), lambda step, shift=shift: (0, step + shift * groups))
        for shift in range(3)
    ]
    square = pl.BlockSpec((group, length, length), lambda step: (step, 0, 0))
    return groups, line, flat, blocks, square


roomy = 40 * 1024 * 1024


def attend(projected, relative, segment):
    heads, length, _ = relative.shape
    model = projected.shape[1] // 3
    groups, line, flat, blocks, square = attention_specs(length, heads, model // heads)
    return pl.pallas_call(
        functools.partial(forward_body, model // heads),
        grid=(groups,),
        in_specs=[line, flat, *blocks, square],
        out_specs=blocks[0],
        out_shape=jax.ShapeDtypeStruct((length, model), jnp.bfloat16),
        compiler_params=pltpu.CompilerParams(vmem_limit_bytes=roomy),
        name="attend",
    )(segment[:, None], segment[None, :], projected, projected, projected, relative)


def attend_back(projected, mixed_grad, relative, segment):
    heads, length, _ = relative.shape
    model = projected.shape[1] // 3
    groups, line, flat, blocks, square = attention_specs(length, heads, model // heads)
    piece = jax.ShapeDtypeStruct((length, model), jnp.bfloat16)
    return pl.pallas_call(
        functools.partial(backward_body, model // heads),
        grid=(groups,),
        in_specs=[line, flat, *blocks, blocks[0], square],
        out_specs=[blocks[0], blocks[0], blocks[0], square],
        out_shape=[piece, piece, piece, jax.ShapeDtypeStruct(relative.shape, jnp.bfloat16)],
        compiler_params=pltpu.CompilerParams(vmem_limit_bytes=roomy),
        name="attend_back",
    )(segment[:, None], segment[None, :], projected, projected, projected, mixed_grad, relative)


def spread_offsets(rows, length):
    heads = rows.shape[0]
    return pl.pallas_call(
        spread_body,
        grid=(heads,),
        in_specs=[pl.BlockSpec((1, 1, 2 * length), lambda head: (head, 0, 0))],
        out_specs=pl.BlockSpec((1, length, length), lambda head: (head, 0, 0)),
        out_shape=jax.ShapeDtypeStruct((heads, length, length), jnp.float32),
        name="spread_offsets",
    )(rows[:, None, :])


def offset_sums(one, two):
    heads, length, _ = one.shape
    square = pl.BlockSpec((1, length, length), lambda head: (head, 0, 0))
    return pl.pallas_call(
        offset_body,
        grid=(heads,),
        in_specs=[square, square],
        out_specs=pl.BlockSpec((1, 1, 2 * length), lambda head: (head, 0, 0)),
        out_shape=jax.ShapeDtypeStruct((heads, 1, 2 * length), jnp.float32),
        name="offset_sums",
    )(one, two)[:, 0, : 2 * length - 1]


def shards(
    ends,
    w_query,
    w_key,
    w_value,
    w_output,
    gain_attention,
    gain_experts,
    router,
    bias_table,
    experts_up,
    experts_down,
    routes,
    slots,
    segments,
    buckets,
):
    section = lax.axis_index(SECTION)
    first = section == 0
    length = (buckets.shape[0] + 1) // 2
    model = ends.shape[2]
    batches = ends.shape[1] // length
    owners = lax.axis_size(EXPERT)
    layers = lax.axis_size(DP)
    mine = lax.axis_index(EXPERT)
    projections = jnp.concatenate([w_query[0], w_key[0], w_value[0], w_output[0]], 1)
    piece = projections.shape[0] // owners
    small = jnp.concatenate(
        [
            gain_attention.reshape(1, -1),
            gain_experts.reshape(1, -1),
            router.reshape(1, -1),
            bias_table.reshape(1, -1),
        ],
        1,
    )
    quarter = lax.all_gather(
        lax.dynamic_slice_in_dim(projections, mine * piece, piece, 0), DP, axis=0
    )

    def spread(block):
        return lax.all_to_all(
            jnp.broadcast_to(block[None], (owners, *block.shape)),
            EXPERT,
            split_axis=0,
            concat_axis=0,
            tiled=True,
        )

    small = lax.all_gather(small, DP, axis=0, tiled=True)
    rows = w_query.shape[1]
    kinds = router.shape[2]
    gain_one = small[:, :rows].reshape(-1).astype(jnp.float32)
    gain_two = small[:, rows : 2 * rows].reshape(-1).astype(jnp.float32)
    router_w = small[:, 2 * rows : (2 + kinds) * rows].reshape(-1, kinds)
    table = small[:, (2 + kinds) * rows :].reshape(-1, bias_table.shape[2]).astype(jnp.float32)
    own_up = experts_up[0]
    own_down = jnp.swapaxes(experts_down[0], 1, 2)
    swapped = lax.ppermute(own_down, SECTION, [(0, 1), (1, 0)])
    own_up, swapped, quarter = lax.optimization_barrier((own_up, swapped, quarter))
    early_w = lax.all_gather(jnp.where(first, own_up, swapped), DP, axis=1, tiled=True)
    late_w = lax.all_gather(jnp.where(first, swapped, own_up), DP, axis=1, tiled=True)
    gathered = jnp.swapaxes(spread(quarter), 0, 1).reshape(layers * owners * piece, -1)
    qkv_w = gathered[:, : 3 * model]
    output_w = gathered[:, 3 * model :]
    local = own_up.shape[0]
    experts = owners * local
    capacity = 2 * length // experts
    heads = table.shape[1]
    bucket_hot = (buckets[None, :] == jnp.arange(table.shape[0], dtype=jnp.int32)[:, None]).astype(
        jnp.float32
    )
    backwards = jnp.concatenate(
        [buckets[:length][::-1], jnp.full((1,), -1, jnp.int32), buckets[length:][::-1]]
    )
    backwards_hot = (
        backwards[None, :] == jnp.arange(table.shape[0], dtype=jnp.int32)[:, None]
    ).astype(jnp.float32)
    relative = spread_offsets(jnp.dot(table.T, backwards_hot, precision=highest), length)
    my_routes = routes[0].reshape(batches, length)
    my_slots = slots[0].reshape(batches, length)
    my_segments = segments.reshape(batches, length)
    data = ends[0].reshape(batches, length, model)
    expert_ids = jnp.arange(experts, dtype=jnp.int32)

    def merged(all_steps):
        ends_step = jax.tree.map(pick, all_steps[batches], all_steps[0])
        return all_steps[1:batches] + [ends_step]

    def product(lefts, rights):
        return sum(
            lax.dot_general(
                left, right, (((0,), (0,)), ((), ())), preferred_element_type=jnp.float32
            )
            for left, right in zip(lefts, rights)
        ).astype(jnp.bfloat16)

    def scatter(values):
        if local == 1:
            return lax.psum_scatter(values[0], DP, scatter_dimension=0, tiled=True)[None]
        return lax.psum_scatter(values, DP, scatter_dimension=1, tiled=True)

    def expert_product(lefts, rights):
        return jnp.stack(
            [
                product(
                    [left[:, one].reshape(-1, left.shape[3]) for left in lefts],
                    [right[:, one].reshape(-1, right.shape[3]) for right in rights],
                )
                for one in range(local)
            ]
        )

    def later_sums(*all_steps):
        return (
            expert_product(
                [each.arrived for each in all_steps], [each.before_grad for each in all_steps]
            ),
            expert_product(
                [each.arrived_grad for each in all_steps], [each.activated for each in all_steps]
            ),
        )

    def empty_sums(*all_steps):
        shape = early_w.shape
        return jnp.zeros(shape, jnp.bfloat16), jnp.zeros(shape, jnp.bfloat16)

    received = jnp.zeros((length, model), jnp.bfloat16)
    stash = []
    produced = []
    for tick in range(batches + 1):
        early = min(tick, batches - 1)
        late = max(tick - 1, 0)
        inputs = jnp.where(first, data[early], received)
        route = jnp.where(first, my_routes[early], my_routes[late])
        slot = jnp.where(first, my_slots[early], my_slots[late])
        segment = jnp.where(first, my_segments[early], my_segments[late])
        current = inputs.astype(jnp.float32)
        forward_normed = normalize(current, gain_one).astype(jnp.bfloat16)
        projected = jnp.dot(forward_normed, qkv_w, preferred_element_type=jnp.float32).astype(
            jnp.bfloat16
        )
        mixed = attend(projected, relative, segment)
        hidden = current + jnp.dot(mixed, output_w, preferred_element_type=jnp.float32)
        routed = normalize(hidden, gain_two).astype(jnp.bfloat16)
        chances = jax.nn.softmax(
            jnp.dot(routed, router_w, preferred_element_type=jnp.float32), axis=-1
        )
        forward_choose = (route[:, None] == expert_ids[None, :]).astype(jnp.float32)
        gate = jnp.sum(chances * forward_choose, axis=-1)
        target = route * capacity + slot
        spots = jnp.arange(experts * capacity, dtype=jnp.int32)
        place = (target[None, :] == spots[:, None]).astype(jnp.bfloat16)
        forward_outgoing = (
            jnp.dot(place, routed, preferred_element_type=jnp.float32)
            .astype(jnp.bfloat16)
            .reshape(owners, local * capacity, model)
        )
        arrived = lax.all_to_all(
            forward_outgoing, EXPERT, split_axis=0, concat_axis=0, tiled=True
        ).reshape(owners, local, capacity, model)
        if tick == 0:
            early_w, arrived = lax.optimization_barrier((early_w, arrived))
            early_down = lax.ppermute(early_w, SECTION, [(1, 0)])
            up_w, down_w = early_w, early_down
        elif tick == 1:
            late_w, arrived = lax.optimization_barrier((late_w, arrived))
            late_down = lax.ppermute(late_w, SECTION, [(0, 1)])
            up_w = jnp.where(first, early_w, late_w)
            down_w = jnp.where(first, early_down, late_down)
        before = jnp.einsum("secd,edf->secf", arrived, up_w, preferred_element_type=jnp.float32)
        activated, slope = gelu_both(before)
        activated, slope = lax.optimization_barrier((activated, slope))
        after = jnp.einsum(
            "secf,edf->secd", activated, down_w, preferred_element_type=jnp.float32
        ).astype(jnp.bfloat16)
        returned = lax.all_to_all(
            after.reshape(owners, local * capacity, model),
            EXPERT,
            split_axis=0,
            concat_axis=0,
            tiled=True,
        ).reshape(experts * capacity, model)
        forward_fetched = jnp.einsum(
            "sl,sd->ld", place, returned, preferred_element_type=jnp.float32
        ).astype(jnp.bfloat16)
        output = hidden + gate[:, None] * forward_fetched.astype(jnp.float32)
        forward_kept = Kept(
            inputs=inputs,
            normed=forward_normed,
            projected=projected,
            mixed=mixed,
            hidden=hidden,
            routed=routed,
            chances=chances,
            gate=gate,
            route=route,
            place=place,
            segment=segment,
            arrived=arrived,
            activated=activated,
            slope=slope,
            fetched=forward_fetched,
        )
        output, kept = (output, forward_kept)
        stash.append(kept)
        produced.append(output.astype(jnp.bfloat16))
        if tick < batches:
            received = from_behind(produced[-1], SECTION, 1)
    def pick(earlier, later):
        return earlier if earlier is later else jnp.where(first, earlier, later)

    steps = []
    expert_steps = []
    arriving = jnp.zeros((length, model), jnp.bfloat16)
    results = []
    for tick in range(batches + 1):
        own = data[min(tick, batches - 1)]
        incoming = jnp.where(first, arriving, own).astype(jnp.float32)
        kept = jax.tree.map(pick, stash[max(tick - 1, 0)], stash[min(tick + 1, batches)])
        if tick == 0:
            kept = stash[min(1, batches)]
        elif tick == batches:
            kept = stash[batches - 1]
        grad_out = incoming
        fetched = kept.fetched.astype(jnp.float32)
        gate_grad = jnp.sum(grad_out * fetched, axis=-1)
        weighted = (kept.gate[:, None] * grad_out).astype(jnp.bfloat16)
        outgoing = (
            jnp.dot(kept.place, weighted, preferred_element_type=jnp.float32)
            .astype(jnp.bfloat16)
            .reshape(owners, local * capacity, model)
        )
        arrived_grad = lax.all_to_all(
            outgoing, EXPERT, split_axis=0, concat_axis=0, tiled=True
        ).reshape(owners, local, capacity, model)
        activation_grad = jnp.einsum(
            "secd,edf->secf", arrived_grad, down_w, preferred_element_type=jnp.float32
        )
        before_grad = (activation_grad * kept.slope.astype(jnp.float32)).astype(jnp.bfloat16)
        if tick == batches:
            early_sum, arrived_grad = lax.optimization_barrier((early_sum, arrived_grad))
            early_share = scatter(early_sum)
        expert_steps.append(ExpertStep(kept.arrived, kept.activated, arrived_grad, before_grad))
        if tick == batches:
            expert_sums = lax.cond(first, later_sums, empty_sums, *expert_steps[1:])
            kept_sums, before_grad = lax.optimization_barrier((expert_sums, before_grad))
            up_sum, down_sum = kept_sums
            swapped = lax.ppermute(down_sum, SECTION, [(0, 1)])
            late_sum = jnp.where(first, up_sum, swapped)
        input_rows_grad = jnp.einsum(
            "secf,edf->secd", before_grad, up_w, preferred_element_type=jnp.float32
        ).astype(jnp.bfloat16)
        back_grad = lax.all_to_all(
            input_rows_grad.reshape(owners, local * capacity, model),
            EXPERT,
            split_axis=0,
            concat_axis=0,
            tiled=True,
        ).reshape(experts * capacity, model)
        routed_grad = jnp.einsum(
            "sl,sd->ld", kept.place, back_grad, preferred_element_type=jnp.float32
        )
        choose = (kept.route[:, None] == expert_ids[None, :]).astype(jnp.float32)
        logit_grad = kept.chances * (
            gate_grad[:, None] * choose - (gate_grad * kept.gate)[:, None]
        )
        routed_full = kept.routed.astype(jnp.float32)
        router_part = jnp.dot(routed_full.T, logit_grad, precision=highest)
        routed_grad = routed_grad + jnp.dot(
            logit_grad, router_w.astype(jnp.float32).T, precision=highest
        )
        second_pull = jax.vjp(normalize, kept.hidden, gain_two)[1]
        hidden_part, gain_two_part = second_pull(routed_grad)
        hidden_grad = grad_out + hidden_part
        branch_grad = hidden_grad.astype(jnp.bfloat16)
        mixed_grad = jnp.einsum(
            "le,ce->lc", branch_grad, output_w, preferred_element_type=jnp.float32
        ).astype(jnp.bfloat16)
        *projected_grad, score_grad = attend_back(
            kept.projected, mixed_grad, relative, kept.segment
        )
        projected_grad = jnp.concatenate(projected_grad, 1)
        if tick == batches:
            early_share, late_sum, projected_grad = lax.optimization_barrier(
                (early_share, late_sum, projected_grad)
            )
            late_share = scatter(late_sum)
        normed_grad = jnp.einsum(
            "le,ce->lc", projected_grad, qkv_w, preferred_element_type=jnp.float32
        )
        first_pull = jax.vjp(normalize, kept.inputs.astype(jnp.float32), gain_one)[1]
        input_part, gain_one_part = first_pull(normed_grad)
        steps.append(
            SharedStep(
                kept.normed,
                kept.mixed,
                branch_grad,
                projected_grad,
                router_part,
                gain_one_part,
                gain_two_part,
                score_grad,
            )
        )
        grad_in = hidden_grad + input_part
        results.append(grad_in.astype(jnp.bfloat16))
        if tick < batches:
            arriving = from_behind(results[-1], SECTION, -1)
        if tick == batches - 1:
            early_sums = lax.cond(first, empty_sums, later_sums, *expert_steps)
            early_sums, arriving = lax.optimization_barrier((early_sums, arriving))
            up_sum, down_sum = early_sums
            swapped = lax.ppermute(down_sum, SECTION, [(1, 0)])
            early_sum = jnp.where(first, swapped, up_sum)
    blocks = [jnp.where(first, results[index + 1], produced[index + 1]) for index in range(batches)]
    ends_out = jnp.concatenate(blocks, 0)[None]
    parts = merged(steps)
    score_pairs = [part.score_grad for part in parts]
    offsets = offset_sums(score_pairs[0], score_pairs[1])
    table_sum = jnp.dot(bucket_hot, offsets.T, precision=highest)
    small_sum = jnp.concatenate(
        [
            sum(part.gain_one for part in parts).reshape(layers, -1),
            sum(part.gain_two for part in parts).reshape(layers, -1),
            sum(part.router for part in parts).reshape(layers, -1),
            table_sum.reshape(layers, -1),
        ],
        1,
    ).astype(jnp.bfloat16)
    extra = 8 - piece % 8
    lines = jnp.pad(small_sum, ((0, 0), (0, extra * 4 * model - small_sum.shape[1])))
    lines = jnp.broadcast_to(
        lines.reshape(layers, 1, extra, 4 * model), (layers, owners, extra, 4 * model)
    )
    projection_sum = jnp.concatenate(
        [
            product([part.normed for part in parts], [part.projected_grad for part in parts]),
            product([part.mixed for part in parts], [part.branch_grad for part in parts]),
        ],
        1,
    ).reshape(layers, owners, piece, 4 * model)
    projection_sum = jnp.concatenate([projection_sum, lines], 2)
    quarters = lax.all_to_all(projection_sum, EXPERT, split_axis=1, concat_axis=1, tiled=True)
    quarter = quarters.astype(jnp.float32).sum(1).astype(jnp.bfloat16)
    late_share, quarter = lax.optimization_barrier((late_share, quarter))
    share = lax.psum_scatter(
        quarter.reshape(layers * (piece + extra), 4 * model), DP, scatter_dimension=0, tiled=True
    )
    shares = spread(share[:piece]).reshape(owners * piece, 4 * model).astype(jnp.float32)
    small_share = share[piece:].reshape(-1).astype(jnp.float32)
    exchanged = lax.ppermute(
        jnp.where(first, early_share, late_share), SECTION, [(0, 1), (1, 0)]
    )
    up_share = jnp.where(first, late_share, early_share).reshape(experts_up.shape)
    down_share = exchanged.reshape(local, -1, own_up.shape[2])
    return (
        ends_out,
        shares[None, :, :model],
        shares[None, :, model : 2 * model],
        shares[None, :, 2 * model : 3 * model],
        shares[None, :, 3 * model :],
        small_share[None, :rows],
        small_share[None, rows : 2 * rows],
        small_share[2 * rows : (2 + kinds) * rows].reshape(1, rows, kinds),
        small_share[(2 + kinds) * rows : small_sum.shape[1]].reshape(1, -1, bias_table.shape[2]),
        up_share.astype(jnp.float32),
        jnp.swapaxes(down_share.astype(jnp.float32), 1, 2)[None],
    )


def solution(mesh):
    in_specs = (
        P(SECTION, (DP, EXPERT), None),
        P(SECTION, DP, None),
        P(SECTION, DP, None),
        P(SECTION, DP, None),
        P(SECTION, DP, None),
        P(SECTION, DP),
        P(SECTION, DP),
        P(SECTION, DP, None),
        P(SECTION, DP, None),
        P(SECTION, EXPERT, DP, None),
        P(SECTION, EXPERT, None, DP),
        P(SECTION, (DP, EXPERT)),
        P(SECTION, (DP, EXPERT)),
        P((DP, EXPERT)),
        P(),
    )
    out_specs = (
        P(SECTION, (DP, EXPERT), None),
        P(SECTION, DP, None),
        P(SECTION, DP, None),
        P(SECTION, DP, None),
        P(SECTION, DP, None),
        P(SECTION, DP),
        P(SECTION, DP),
        P(SECTION, DP, None),
        P(SECTION, DP, None),
        P(SECTION, EXPERT, DP, None),
        P(SECTION, EXPERT, None, DP),
    )
    return jax.shard_map(shards, mesh=mesh, in_specs=in_specs, out_specs=out_specs, check_vma=False)
```
